512 devices in a mesh: blk: 64 (over z_lo, x, core), uly: 8 (over z_hi, y).
Axes of the slice: x: 4, y: 4, z: 16 (z_hi: 2, z_lo: 8; z = z_hi * 8 + z_lo), core: 2. Of those that a mesh axis runs over, the one named last changes fastest.
Arguments:
- query_in: bfloat16 [64, 1024, 2048], P('blk', 'uly'), may hold values from -54 to 54
- key_in: bfloat16 [64, 1024, 2048], P('blk', 'uly'), may hold values from -54 to 54
- value_in: bfloat16 [64, 1024, 2048], P('blk', 'uly'), may hold values from -12 to 12
- velocity_grad: bfloat16 [64, 1024, 3072], P('blk', 'uly'), may hold values from -108 to 108
- velocity_gap: bfloat16 [64, 1024, 3072], P('blk', 'uly'), may hold values from -6 to 6
- query_gain: float32 [128], replicated, may hold values from 1 to 6.5
- key_gain: float32 [128], replicated, may hold values from 1 to 6.5
- out_proj: bfloat16 [2048, 3072], P('uly', 'blk'), may hold values from -0.125 to 0.125
Outputs:
- grad_query: bfloat16 [64, 1024, 2048], P('blk', 'uly')
- grad_key: bfloat16 [64, 1024, 2048], P('blk', 'uly')
- grad_value: bfloat16 [64, 1024, 2048], P('blk', 'uly')
- gain_grads: float32 [2, 128], replicated
- grad_out_proj: float32 [2048, 3072], P('uly', 'blk')
The draws below stay inside these ranges and needn't reach their ends.
All inputs are finite; a program needn't handle non-finite values.
Results may differ from the reference program's by a relative error of at most 0.0095.
The reference program's roundings to bfloat16 on the way count: a program that leaves them out, or rounds other values in their place, can miss the bound.
Values may be sent and summed in bfloat16 or wider, within the bound.
No kernel may reach another device: no remote copies, remote signals or barrier semaphores. Data moves between devices by JAX's collectives and lax.ppermute only.
A program may use at most 64 MiB of HBM per device.

```python
import math
import jax
import jax.numpy as jnp
from jax import lax

D = 3072
H = 16
HD = 128
SEQ = 1024
SAMPLES = 64


def paired_rows(key, first):
    width_all = H * HD
    row_total = SAMPLES * SEQ
    query_key = jax.random.fold_in(key, first)
    other_key = jax.random.fold_in(key, first + 1)
    raw_query = jax.random.truncated_normal(query_key, -3.0, 3.0, (row_total, width_all), jnp.float32)
    raw_other = jax.random.truncated_normal(other_key, -3.0, 3.0, (row_total, width_all), jnp.float32)
    row_query = jnp.exp(jax.random.uniform(jax.random.fold_in(key, first + 2), (row_total, 1), jnp.float32, math.log(0.6), math.log(6.0)))
    row_other = jnp.exp(jax.random.uniform(jax.random.fold_in(key, first + 3), (row_total, 1), jnp.float32, math.log(0.6), math.log(6.0)))
    column_scale = jnp.exp(jax.random.uniform(jax.random.fold_in(key, first + 4), (1, width_all), jnp.float32, math.log(0.3), math.log(3.0)))
    queries = raw_query * row_query * column_scale
    keyset = raw_other * row_other * column_scale
    return (queries.reshape(SAMPLES, SEQ, width_all), keyset.reshape(SAMPLES, SEQ, width_all))


def gain_law(key):
    return jnp.exp(jax.random.uniform(key, (HD,), jnp.float32, 0.0, math.log(3.0)))


def draw_query_in(key, part):
    queries, keyset = paired_rows(key, 10)
    return queries.astype(jnp.bfloat16)


def draw_key_in(key, part):
    queries, keyset = paired_rows(key, 10)
    return keyset.astype(jnp.bfloat16)


def draw_velocity_grad(key, part):
    key = jax.random.fold_in(key, 41)
    shape_all = (SAMPLES, SEQ, D)
    base = jax.random.truncated_normal(jax.random.fold_in(key, 1), -3.0, 3.0, shape_all, jnp.float32)
    top_scale = math.log(3.0)
    sample_scale = jnp.exp(jnp.linspace(0.0, top_scale, SAMPLES)).reshape(SAMPLES, 1, 1)
    owner = jax.random.permutation(jax.random.fold_in(key, 3), SAMPLES)
    column_block = jnp.arange(D) // (D // SAMPLES)
    boost = jnp.where(column_block[None, :] == owner[:, None], 4.0, 1.0)[:, None, :]
    return (base * sample_scale * boost).astype(jnp.bfloat16)


def draw_query_gain(key, part):
    key = jax.random.fold_in(key, 31)
    return gain_law(key)


def draw_key_gain(key, part):
    key = jax.random.fold_in(key, 32)
    return gain_law(key)


def block_levels(rng, dims, shards, least, top_value):
    def one(axis_at, shards_of):
        heights = jax.random.uniform(jax.random.fold_in(jax.random.fold_in(rng, 6), axis_at), (shards_of,), jnp.float32, least / len(shards), top_value / len(shards))
        return jnp.repeat(jnp.exp(heights), dims[axis_at] // shards_of).reshape((-1,) + (1,) * (len(dims) - axis_at - 1))

    loudness = one(*shards[0])
    for cut in shards[1:]:
        loudness = loudness * one(*cut)
    return loudness


def bell_draw(stream_key, extent, width, bound, pieces=(), kind=jnp.bfloat16):
    level = block_levels(stream_key, extent, pieces, -0.22, 0.18) if pieces else 1.0
    entries = jax.random.normal(stream_key, extent, jnp.float32) * width * level
    return jnp.minimum(jnp.maximum(entries, -bound), bound).astype(kind)


def setup_inputs(seed: int = 0) -> dict:
    splits = jax.random.split(jax.random.key(seed), 9)
    query_in = draw_query_in(jax.random.fold_in(splits[8], 71), 0)
    key_in = draw_key_in(jax.random.fold_in(splits[8], 71), 0)
    value_in = bell_draw(splits[2], (SAMPLES, SEQ, H * HD), 2.0, 12.0, ((0, 64), (1, 8)))
    velocity_grad = draw_velocity_grad(jax.random.fold_in(splits[8], 71), 0)
    velocity_gap = bell_draw(splits[4], (SAMPLES, SEQ, D), 1.0, 6.0, ((0, 64), (1, 8)))
    query_gain = draw_query_gain(jax.random.fold_in(splits[8], 71), 0)
    key_gain = draw_key_gain(jax.random.fold_in(splits[8], 71), 0)
    out_proj = bell_draw(splits[7], (H * HD, D), (H * HD) ** -0.5, 0.125, ((0, 8), (1, 64)))
    return {"query_in": query_in, "key_in": key_in, "value_in": value_in, "velocity_grad": velocity_grad, "velocity_gap": velocity_gap, "query_gain": query_gain, "key_gain": key_gain, "out_proj": out_proj}


kl_weight = 0.5
norm_eps = 1e-06

def head_norm(field, gain):
    mean_square = lax.optimization_barrier(jnp.mean(field * field, axis=-1, keepdims=True))
    return field * lax.rsqrt(mean_square + norm_eps) * gain

def attend_head(inputs):
    queries, keyset, valueset = inputs
    score_scale = 1.0 / math.sqrt(HD)
    scores = jnp.dot(queries, keyset.T, preferred_element_type=jnp.float32) * score_scale
    row_top = lax.optimization_barrier(jnp.max(scores, axis=1, keepdims=True))
    log_total = row_top + jnp.log(lax.optimization_barrier(jnp.sum(jnp.exp(scores - row_top), axis=1, keepdims=True)))
    weights = jnp.exp(scores - log_total).astype(jnp.bfloat16)
    outcome = jnp.dot(weights, valueset, preferred_element_type=jnp.float32).astype(jnp.bfloat16)
    return (outcome, log_total)

def backward_head(inputs):
    queries, keyset, valueset, outcome, d_outcome, log_total = inputs
    score_scale = 1.0 / math.sqrt(HD)
    scores = jnp.dot(queries, keyset.T, preferred_element_type=jnp.float32) * score_scale
    weights = jnp.exp(scores - log_total)
    delta_rows = lax.optimization_barrier(jnp.sum(d_outcome.astype(jnp.float32) * outcome.astype(jnp.float32), axis=1, keepdims=True))
    d_weights = jnp.dot(d_outcome, valueset.T, preferred_element_type=jnp.float32)
    d_scores = (weights * (d_weights - delta_rows)).astype(jnp.bfloat16)
    d_query = jnp.dot(d_scores, keyset, preferred_element_type=jnp.float32) * score_scale
    d_key = jnp.dot(d_scores.T, queries, preferred_element_type=jnp.float32) * score_scale
    d_value = jnp.dot(weights.astype(jnp.bfloat16).T, d_outcome, preferred_element_type=jnp.float32)
    return (d_query, d_key, d_value)

def by_head(field):
    return jnp.transpose(field.reshape(SEQ, H, HD), (1, 0, 2))

def by_token(field):
    return jnp.transpose(field, (1, 0, 2)).reshape(SEQ, H * HD)

def reference(query_in, key_in, value_in, velocity_grad, velocity_gap, query_gain, key_gain, out_proj):

    def sample_pass(running, inputs):
        gain_acc, weight_acc = running
        query_s, key_s, value_s, vgrad_s, vgap_s = inputs
        query_f = by_head(query_s).astype(jnp.float32)
        key_f = by_head(key_s).astype(jnp.float32)
        query_n = head_norm(query_f, query_gain).astype(jnp.bfloat16)
        key_n = head_norm(key_f, key_gain).astype(jnp.bfloat16)
        value_h = by_head(value_s)
        outcome, log_total = lax.map(attend_head, (query_n, key_n, value_h))
        d_velocity = (vgrad_s.astype(jnp.float32) + kl_weight * vgap_s.astype(jnp.float32)).astype(jnp.bfloat16)
        d_outcome = jnp.dot(d_velocity, out_proj.T, preferred_element_type=jnp.float32).astype(jnp.bfloat16)
        weight_acc = weight_acc + jnp.dot(by_token(outcome).T, d_velocity, preferred_element_type=jnp.float32)
        d_query_n, d_key_n, d_value = lax.map(backward_head, (query_n, key_n, value_h, outcome, by_head(d_outcome), log_total))
        unused_q, pull_query = jax.vjp(head_norm, query_f, query_gain)
        grad_query_f, query_gain_grad = pull_query(d_query_n)
        unused_k, pull_key = jax.vjp(head_norm, key_f, key_gain)
        grad_key_f, key_gain_grad = pull_key(d_key_n)
        gain_acc = gain_acc + jnp.stack([query_gain_grad, key_gain_grad])
        grads = (by_token(grad_query_f).astype(jnp.bfloat16), by_token(grad_key_f).astype(jnp.bfloat16), by_token(d_value).astype(jnp.bfloat16))
        return ((gain_acc, weight_acc), grads)
    initial = (jnp.zeros((2, HD), jnp.float32), jnp.zeros((H * HD, D), jnp.float32))
    totals, grads = lax.scan(sample_pass, initial, (query_in, key_in, value_in, velocity_grad, velocity_gap))
    return (grads[0], grads[1], grads[2], totals[0], totals[1])
```

```python
import itertools
import math

import jax
import jax.numpy as jnp
import numpy as np
from jax import lax
from jax.experimental import pallas as pl
from jax.experimental.pallas import tpu as pltpu
from jax.sharding import Mesh, PartitionSpec as P

kl_weight = 0.5
norm_eps = 1e-06

AXES = ("zlo", "x", "core", "zhi", "y")
SIZES = (8, 4, 2, 2, 4)
PLACES = list(itertools.product(*map(range, SIZES)))
BF = jnp.bfloat16
F32 = jnp.float32
HEAD = 128
ROWS = 128
GROUPS = 8
SEQ = GROUPS * ROWS
TILE = 256
BLOCK = 96


def moved(field, where):
    number = lambda place: int(np.ravel_multi_index(place, SIZES))
    pairs = [(number(place), number(where(*place))) for place in PLACES]
    return lax.ppermute(field, AXES, pairs)


def clip_swap(l, x, c, h, y):
    return (l, x, h, c, y)


def clip_cross(l, x, c, h, y):
    return (l, x, 1 - h, c, y)


def core_swap(l, x, c, h, y):
    return (l, x, 1 - c, h, y)


def y_step(step):
    return lambda l, x, c, h, y: (l, x, c, h, (y + step) % 4)


def x_step(step):
    return lambda l, x, c, h, y: (l, x ^ step, c, h, y)


def whole():
    return pl.BlockSpec(memory_space=pltpu.VMEM)


def anywhere():
    return pl.BlockSpec(memory_space=pl.ANY)


def after(field, *earlier):
    return pl.pallas_call(
        lambda *refs: None,
        out_shape=jax.ShapeDtypeStruct(field.shape, field.dtype),
        in_specs=[anywhere()] * (1 + len(earlier)),
        out_specs=anywhere(),
        input_output_aliases={0: 0},
    )(field, *earlier)


def prepare_kernel(query_ref, key_ref, value_ref, first_ref, second_ref):
    for part, ref in enumerate((query_ref, key_ref, value_ref)):
        for group in range(GROUPS):
            at = group * 2 * HEAD
            first_ref[group, part] = ref[:, at : at + HEAD]
            second_ref[group, part] = ref[:, at + HEAD : at + 2 * HEAD]


def prepare(query, key, value):
    shape = jax.ShapeDtypeStruct((GROUPS, 3, ROWS, HEAD), BF)
    return pl.pallas_call(
        prepare_kernel,
        out_shape=(shape, shape),
        in_specs=[whole()] * 3,
        out_specs=(whole(), whole()),
    )(query, key, value)


def finish_kernel(first_ref, second_ref, query_ref, key_ref, value_ref):
    for part, ref in enumerate((query_ref, key_ref, value_ref)):
        for group in range(GROUPS):
            at = group * 2 * HEAD
            ref[:, at : at + HEAD] = first_ref[group, part]
            ref[:, at + HEAD : at + 2 * HEAD] = second_ref[group, part]


def finish(first, second):
    shape = jax.ShapeDtypeStruct((ROWS, GROUPS * 2 * HEAD), BF)
    return pl.pallas_call(
        finish_kernel,
        out_shape=(shape,) * 3,
        in_specs=[whole()] * 2,
        out_specs=(whole(),) * 3,
    )(first, second)


def project_kernel(order_ref, *refs):
    blocks, weight_ref, out_ref, rows, sems = refs[:8], refs[8], refs[9], refs[10], refs[11]
    copies = [
        pltpu.make_async_copy(blocks[i], rows.at[order_ref[i]], sems.at[i]) for i in range(8)
    ]
    for copy in copies:
        copy.start()
    for copy in copies:
        copy.wait()
    width = rows.shape[-1]
    out = jnp.dot(
        rows[...].reshape(SEQ, width), weight_ref[...], preferred_element_type=F32
    ).astype(BF)
    for head in range(2):
        out_ref[head] = out[:, head * HEAD : (head + 1) * HEAD]


def project(order, blocks, weight):
    width = weight.shape[0]
    return pl.pallas_call(
        project_kernel,
        out_shape=jax.ShapeDtypeStruct((2, SEQ, HEAD), BF),
        in_specs=[pl.BlockSpec(memory_space=pltpu.SMEM)] + [anywhere()] * 8 + [whole()],
        out_specs=whole(),
        scratch_shapes=[
            pltpu.VMEM((GROUPS, ROWS, width), BF),
            pltpu.SemaphoreType.DMA((8,)),
        ],
        compiler_params=pltpu.CompilerParams(vmem_limit_bytes=40 << 20),
        cost_estimate=pl.CostEstimate(
            flops=2 * SEQ * width * 256, bytes_accessed=10 << 20, transcendentals=0
        ),
    )(order, *blocks, weight)


def attend_kernel(head, in_ref, d_out_ref, gain_ref, out_ref, grad_ref, gain_out_ref, dk_acc, dv_acc, dq_all):
    scale = 1.0 / math.sqrt(HEAD)
    query_f = in_ref[:, 0].reshape(SEQ, HEAD).astype(F32)
    key_f = in_ref[:, 1].reshape(SEQ, HEAD).astype(F32)
    value = in_ref[:, 2].reshape(SEQ, HEAD)
    query_gain = gain_ref[0:1]
    key_gain = gain_ref[1:2]
    query_r = lax.rsqrt(jnp.mean(query_f * query_f, axis=-1, keepdims=True) + norm_eps)
    key_r = lax.rsqrt(jnp.mean(key_f * key_f, axis=-1, keepdims=True) + norm_eps)
    query_n = (query_f * query_r * query_gain).astype(BF)
    key_n = (key_f * key_r * key_gain).astype(BF)
    key_t = key_n.T
    value_t = value.T
    for tile in range(SEQ // TILE):
        at = tile * TILE
        query_tile = query_n[at : at + TILE]
        d_out = d_out_ref[head, at : at + TILE]
        d_out_t = d_out.T
        scores = jnp.dot(key_n, query_tile.T, preferred_element_type=F32) * scale
        top = jnp.max(scores, axis=0, keepdims=True)
        terms = jnp.exp(scores - top)
        weights = terms * (1.0 / jnp.sum(terms, axis=0, keepdims=True))
        weights_b = weights.astype(BF)
        out_t = jnp.dot(value_t, weights_b, preferred_element_type=F32).astype(BF)
        delta = jnp.sum(d_out_t.astype(F32) * out_t.astype(F32), axis=0, keepdims=True)
        d_weights = jnp.dot(value, d_out_t, preferred_element_type=F32)
        d_scores = (weights * (d_weights - delta)).astype(BF)
        d_query_t = jnp.dot(key_t, d_scores, preferred_element_type=F32)
        d_key = jnp.dot(d_scores, query_tile, preferred_element_type=F32)
        d_value = jnp.dot(weights_b, d_out, preferred_element_type=F32)
        out_ref[at : at + TILE] = out_t.T
        dq_all[at : at + TILE] = d_query_t.T
        if tile == 0:
            dk_acc[...] = d_key
            dv_acc[...] = d_value
        else:
            dk_acc[...] += d_key
            dv_acc[...] += d_value

    def pull(field, r, gain, cotangent):
        cotangent = cotangent * scale
        scaled = field * r
        gained = cotangent * gain
        inner = jnp.mean(gained * scaled, axis=-1, keepdims=True)
        grad = (r * (gained - scaled * inner)).astype(BF)
        return grad.reshape(GROUPS, ROWS, HEAD), jnp.sum(cotangent * scaled, axis=0, keepdims=True)

    grad_ref[:, 0], query_part = pull(query_f, query_r, query_gain, dq_all[...])
    grad_ref[:, 1], key_part = pull(key_f, key_r, key_gain, dk_acc[...])
    grad_ref[:, 2] = dv_acc[...].astype(BF).reshape(GROUPS, ROWS, HEAD)
    gain_out_ref[...] = jnp.concatenate([query_part, key_part], axis=0)


def attend(head, fields, d_out, gains):
    return pl.pallas_call(
        lambda *refs: attend_kernel(head, *refs),
        out_shape=(
            jax.ShapeDtypeStruct((SEQ, HEAD), BF),
            jax.ShapeDtypeStruct((GROUPS, 3, ROWS, HEAD), BF),
            jax.ShapeDtypeStruct((2, HEAD), F32),
        ),
        in_specs=[whole()] * 3,
        out_specs=(whole(),) * 3,
        scratch_shapes=[pltpu.VMEM((SEQ, HEAD), F32)] * 3,
        compiler_params=pltpu.CompilerParams(vmem_limit_bytes=40 << 20),
        cost_estimate=pl.CostEstimate(
            flops=12 * SEQ * SEQ * HEAD, bytes_accessed=2 << 20, transcendentals=SEQ * SEQ
        ),
    )(fields, d_out, gains)


def pair_rows(row):
    high = row.astype(BF)
    low = (row - high.astype(F32)).astype(BF)
    return jnp.concatenate([high, low, jnp.zeros((14, row.shape[1]), BF)], axis=0)


def weigh_kernel(order_ref, *refs):
    blocks = refs[:8]
    first_ref, second_ref, gain_first, gain_second, out_ref, rows, sems = refs[8:]
    copies = [
        pltpu.make_async_copy(blocks[i], rows.at[order_ref[i]], sems.at[i]) for i in range(8)
    ]
    for copy in copies:
        copy.start()
    for copy in copies:
        copy.wait()
    step = 8 * BLOCK
    for head, ref in enumerate((first_ref, second_ref)):
        out_t = ref[...].T
        for part in range(rows.shape[-1] // step):
            columns = rows[:, :, part * step : (part + 1) * step].reshape(SEQ, step)
            term = jnp.dot(out_t, columns, preferred_element_type=F32).T.astype(BF)
            for i in range(8):
                out_ref[i % 4, 2 * part + i // 4, 0:BLOCK, head * HEAD : (head + 1) * HEAD] = term[
                    i * BLOCK : (i + 1) * BLOCK
                ]
    gains = gain_first[...] + gain_second[...]
    tail = pair_rows(jnp.concatenate([gains[0:1], gains[1:2]], axis=1))
    for i in range(4):
        for j in range(8):
            out_ref[i, j, BLOCK : BLOCK + 16] = tail


def weigh(order, blocks, outs, gain_parts):
    width = blocks[0].shape[-1]
    return pl.pallas_call(
        weigh_kernel,
        out_shape=jax.ShapeDtypeStruct((4, 8, BLOCK + 16, 2 * HEAD), BF),
        in_specs=[pl.BlockSpec(memory_space=pltpu.SMEM)] + [anywhere()] * 8 + [whole()] * 4,
        out_specs=whole(),
        scratch_shapes=[
            pltpu.VMEM((GROUPS, ROWS, width), BF),
            pltpu.SemaphoreType.DMA((8,)),
        ],
        compiler_params=pltpu.CompilerParams(vmem_limit_bytes=40 << 20),
        cost_estimate=pl.CostEstimate(
            flops=2 * SEQ * width * 256, bytes_accessed=10 << 20, transcendentals=0
        ),
    )(order, *blocks, *outs, *gain_parts)


def first_sum_kernel(in_ref, out_ref):
    for j in range(8):
        total = sum(in_ref[i, j].astype(F32) for i in range(4))
        out_ref[j, 0:BLOCK] = total[0:BLOCK].astype(BF)
        out_ref[j, BLOCK : BLOCK + 16] = pair_rows(
            total[BLOCK : BLOCK + 1] + total[BLOCK + 1 : BLOCK + 2]
        )


def first_sum(field):
    return pl.pallas_call(
        first_sum_kernel,
        out_shape=jax.ShapeDtypeStruct(field.shape[1:], BF),
        in_specs=[whole()],
        out_specs=whole(),
    )(field)


def second_sum_kernel(in_ref, out_ref, gain_ref):
    total = sum(in_ref[j].astype(F32) for j in range(8))
    out_ref[0] = total[0 : BLOCK // 2]
    out_ref[1] = total[BLOCK // 2 : BLOCK]
    gain = total[BLOCK : BLOCK + 1] + total[BLOCK + 1 : BLOCK + 2]
    gain_ref[...] = jnp.broadcast_to(gain[None], gain_ref.shape)


def second_sum(field):
    return pl.pallas_call(
        second_sum_kernel,
        out_shape=(
            jax.ShapeDtypeStruct((2, BLOCK // 2, 2 * HEAD), F32),
            jax.ShapeDtypeStruct((8, 8, 2 * HEAD), F32),
        ),
        in_specs=[whole()],
        out_specs=(whole(), whole()),
    )(field)


def local(query_in, key_in, value_in, velocity_grad, velocity_gap, query_gain, key_gain, out_proj):
    core, zhi, y = lax.axis_index("core"), lax.axis_index("zhi"), lax.axis_index("y")
    d_velocity = (
        velocity_grad[0].astype(F32) + kl_weight * velocity_gap[0].astype(F32)
    ).astype(BF)
    d_velocity = moved(d_velocity, clip_swap)
    first, second = prepare(query_in[0], key_in[0], value_in[0])

    own = out_proj.T
    other = moved(own, core_swap)
    low = jnp.where(core == 0, own, other)
    high = jnp.where(core == 0, other, own)
    columns = moved(jnp.concatenate([low, high], axis=0), clip_swap)
    columns = lax.all_to_all(
        jnp.broadcast_to(columns[None], (8,) + columns.shape), "zlo", 0, 0
    )
    columns = lax.all_gather(columns, "x", axis=1)
    weight = columns.reshape(-1, 2 * HEAD)

    blocks = [d_velocity] + [moved(d_velocity, y_step(step)) for step in (1, 3, 2)]
    blocks = blocks + [moved(block, core_swap) for block in blocks]
    from_y = [y, (y + 3) % 4, (y + 1) % 4, (y + 2) % 4]
    order = jnp.stack([core * 4 + at for at in from_y] + [(1 - core) * 4 + at for at in from_y])
    order = order.astype(jnp.int32)
    gains = jnp.stack([query_gain, key_gain])

    first = moved(after(first, d_velocity), clip_swap)
    first_in = lax.all_to_all(first, ("core", "y"), 0, 0)
    second = moved(after(second, first), clip_swap)
    d_out = project(order, blocks, weight)
    first_out, first_grad, first_gain = attend(0, first_in, d_out, gains)
    first_back = lax.all_to_all(first_grad, ("core", "y"), 0, 0)
    first_back = moved(first_back, clip_swap)
    second_in = lax.all_to_all(second, ("core", "y"), 0, 0)
    second_out, second_grad, second_gain = attend(1, second_in, d_out, gains)
    second_back = lax.all_to_all(second_grad, ("core", "y"), 0, 0)
    second_back = moved(second_back, clip_swap)

    terms = weigh(order, blocks, (first_out, second_out), (first_gain, second_gain))
    terms = first_sum(lax.all_to_all(terms, "x", 0, 0))
    halves, gain_rows = second_sum(lax.all_to_all(terms, "zlo", 0, 0))
    gain_rows = jnp.sum(lax.all_to_all(gain_rows, ("core", "y"), 0, 0), axis=0)
    straight = jnp.where(zhi == 0, halves[0], halves[1])
    across = jnp.where(zhi == 0, halves[1], halves[0])
    straight = moved(jnp.concatenate([straight, gain_rows], axis=0), clip_swap)
    across = moved(jnp.concatenate([across, gain_rows], axis=0), clip_cross)
    total = straight + across
    grad_out_proj = total[: BLOCK // 2].T
    gain_grads = total[BLOCK // 2].reshape(2, HEAD)

    grad_query, grad_key, grad_value = finish(first_back, second_back)
    return (grad_query[None], grad_key[None], grad_value[None], gain_grads, grad_out_proj)


def solution(mesh):
    fine = Mesh(mesh.devices.reshape(SIZES), AXES)
    blk, uly = ("zlo", "x", "core"), ("zhi", "y")
    rows = P(blk, uly, None)
    return jax.shard_map(
        local,
        mesh=fine,
        in_specs=(rows, rows, rows, rows, rows, P(), P(), P(uly, blk)),
        out_specs=(rows, rows, rows, P(), P(uly, blk)),
        check_vma=False,
    )
```

```python
import itertools
import math

import jax
import jax.numpy as jnp
import numpy as np
from jax import lax
from jax.experimental import pallas as pl
from jax.experimental.pallas import tpu as pltpu
from jax.sharding import Mesh, PartitionSpec as P

kl_weight = 0.5
norm_eps = 1e-06

AXES = ("zlo", "x", "core", "zhi", "y")
SIZES = (8, 4, 2, 2, 4)
PLACES = list(itertools.product(*map(range, SIZES)))
BF = jnp.bfloat16
F32 = jnp.float32
HEAD = 128
ROWS = 128
GROUPS = 8
SEQ = GROUPS * ROWS
TILE = 256
BLOCK = 96
PARTS = 12


def moved(field, where):
    number = lambda place: int(np.ravel_multi_index(place, SIZES))
    pairs = [(number(place), number(where(*place))) for place in PLACES]
    return lax.ppermute(field, AXES, pairs)


def clip_swap(l, x, c, h, y):
    return (l, x, h, c, y)


def clip_cross(l, x, c, h, y):
    return (l, x, 1 - h, c, y)


def core_swap(l, x, c, h, y):
    return (l, x, 1 - c, h, y)


def y_step(step):
    return lambda l, x, c, h, y: (l, x, c, h, (y + step) % 4)


def x_step(step):
    return lambda l, x, c, h, y: (l, x ^ step, c, h, y)


def z_pair(step):
    return lambda l, x, c, h, y: (l ^ step, x, c, h, y)


def whole():
    return pl.BlockSpec(memory_space=pltpu.VMEM)


def anywhere():
    return pl.BlockSpec(memory_space=pl.ANY)


def after(field, *earlier):
    return pl.pallas_call(
        lambda *refs: None,
        out_shape=jax.ShapeDtypeStruct(field.shape, field.dtype),
        in_specs=[anywhere()] * (1 + len(earlier)),
        out_specs=anywhere(),
        input_output_aliases={0: 0},
    )(field, *earlier)


def prepare_kernel(query_ref, key_ref, value_ref, first_ref, second_ref):
    for part, ref in enumerate((query_ref, key_ref, value_ref)):
        for group in range(GROUPS):
            at = group * 2 * HEAD
            first_ref[group, part] = ref[:, at : at + HEAD]
            second_ref[group, part] = ref[:, at + HEAD : at + 2 * HEAD]


def prepare(query, key, value):
    shape = jax.ShapeDtypeStruct((GROUPS, 3, ROWS, HEAD), BF)
    return pl.pallas_call(
        prepare_kernel,
        out_shape=(shape, shape),
        in_specs=[whole()] * 3,
        out_specs=(whole(), whole()),
    )(query, key, value)


def finish_kernel(first_ref, second_ref, query_ref, key_ref, value_ref):
    for part, ref in enumerate((query_ref, key_ref, value_ref)):
        rows = slice(part * ROWS, (part + 1) * ROWS)
        for group in range(GROUPS):
            at = group * 2 * HEAD
            ref[:, at : at + HEAD] = first_ref[group, rows]
            ref[:, at + HEAD : at + 2 * HEAD] = second_ref[group, rows]


def finish(first, second):
    shape = jax.ShapeDtypeStruct((ROWS, GROUPS * 2 * HEAD), BF)
    return pl.pallas_call(
        finish_kernel,
        out_shape=(shape,) * 3,
        in_specs=[whole()] * 2,
        out_specs=(whole(),) * 3,
    )(first, second)


def form_kernel(core_ref, grad_ref, gap_ref, own_ref, other_ref, out_ref):
    for j in range(PARTS):
        at = slice(j * 256, (j + 1) * 256)
        out_ref[j * ROWS : (j + 1) * ROWS] = (
            grad_ref[:, at].astype(F32) + kl_weight * gap_ref[:, at].astype(F32)
        ).astype(BF)
    half = BLOCK // 2
    core = core_ref[0]
    own_at = pl.multiple_of(PARTS * ROWS + core * half, 16)
    other_at = pl.multiple_of(PARTS * ROWS + (1 - core) * half, 16)
    out_ref[pl.ds(own_at, half)] = own_ref[...]
    out_ref[pl.ds(other_at, half)] = other_ref[...]


def form(core, grad, gap, own, other):
    return pl.pallas_call(
        form_kernel,
        out_shape=jax.ShapeDtypeStruct((PARTS * ROWS + BLOCK, 256), BF),
        in_specs=[pl.BlockSpec(memory_space=pltpu.SMEM)] + [whole()] * 4,
        out_specs=whole(),
    )(core, grad, gap, own, other)


def gather_blocks(order_ref, blocks, rows, sems):
    copies = [
        pltpu.make_async_copy(blocks[i], rows.at[:, order_ref[i]], sems.at[i]) for i in range(8)
    ]
    for copy in copies:
        copy.start()
    for copy in copies:
        copy.wait()


def block_scratch():
    return [pltpu.VMEM((PARTS, GROUPS, ROWS, 256), BF), pltpu.SemaphoreType.DMA((8,))]


def project_kernel(order_ref, *refs):
    blocks, weight_ref, out_ref, rows, sems = refs[:8], refs[8], refs[9], refs[10], refs[11]
    gather_blocks(order_ref, blocks, rows, sems)
    for pair in range(4):
        total = None
        for j in range(PARTS):
            part = jnp.dot(
                rows[j, 2 * pair : 2 * pair + 2].reshape(2 * ROWS, 256),
                weight_ref[j * 256 : (j + 1) * 256],
                preferred_element_type=F32,
            )
            total = part if total is None else total + part
        out = total.astype(BF)
        at = pair * 2 * ROWS
        for head in range(2):
            out_ref[head, at : at + 2 * ROWS] = out[:, head * HEAD : (head + 1) * HEAD]


def project(order, blocks, weight):
    return pl.pallas_call(
        project_kernel,
        out_shape=jax.ShapeDtypeStruct((2, SEQ, HEAD), BF),
        in_specs=[pl.BlockSpec(memory_space=pltpu.SMEM)] + [anywhere()] * 8 + [whole()],
        out_specs=whole(),
        scratch_shapes=block_scratch(),
        compiler_params=pltpu.CompilerParams(vmem_limit_bytes=40 << 20),
    )(order, *blocks, weight)


def attend_kernel(head, *refs):
    in_ref, d_out_ref, gain_ref = refs[:3]
    earlier_ref = refs[3] if len(refs) == 10 else None
    out_ref, grad_ref, gain_out_ref, dk_acc, dv_acc, dq_all = refs[-6:]
    scale = 1.0 / math.sqrt(HEAD)
    query_f = in_ref[:, 0].reshape(SEQ, HEAD).astype(F32)
    key_f = in_ref[:, 1].reshape(SEQ, HEAD).astype(F32)
    value = in_ref[:, 2].reshape(SEQ, HEAD)
    query_gain = gain_ref[0:1]
    key_gain = gain_ref[1:2]
    query_r = lax.rsqrt(jnp.mean(query_f * query_f, axis=-1, keepdims=True) + norm_eps)
    key_r = lax.rsqrt(jnp.mean(key_f * key_f, axis=-1, keepdims=True) + norm_eps)
    query_n = (query_f * query_r * query_gain).astype(BF)
    key_n = (key_f * key_r * key_gain).astype(BF)
    key_t = key_n.T
    value_t = value.T
    for tile in range(SEQ // TILE):
        at = tile * TILE
        query_tile = query_n[at : at + TILE]
        d_out = d_out_ref[head, at : at + TILE]
        d_out_t = d_out.T
        scores = jnp.dot(key_n, query_tile.T, preferred_element_type=F32) * scale
        top = jnp.max(scores, axis=0, keepdims=True)
        terms = jnp.exp(scores - top)
        weights = terms * (1.0 / jnp.sum(terms, axis=0, keepdims=True))
        weights_b = weights.astype(BF)
        out_t = jnp.dot(value_t, weights_b, preferred_element_type=F32).astype(BF)
        delta = jnp.sum(d_out_t.astype(F32) * out_t.astype(F32), axis=0, keepdims=True)
        d_weights = jnp.dot(value, d_out_t, preferred_element_type=F32)
        d_scores = (weights * (d_weights - delta)).astype(BF)
        d_query_t = jnp.dot(key_t, d_scores, preferred_element_type=F32)
        d_key = jnp.dot(d_scores, query_tile, preferred_element_type=F32)
        d_value = jnp.dot(weights_b, d_out, preferred_element_type=F32)
        out_ref[at : at + TILE] = out_t.T
        dq_all[at : at + TILE] = d_query_t.T
        if tile == 0:
            dk_acc[...] = d_key
            dv_acc[...] = d_value
        else:
            dk_acc[...] += d_key
            dv_acc[...] += d_value

    def pull(field, r, gain, cotangent):
        cotangent = cotangent * scale
        scaled = field * r
        gained = cotangent * gain
        inner = jnp.mean(gained * scaled, axis=-1, keepdims=True)
        grad = (r * (gained - scaled * inner)).astype(BF)
        return grad.reshape(GROUPS, ROWS, HEAD), jnp.sum(cotangent * scaled, axis=0, keepdims=True)

    grad_ref[:, 0:ROWS], query_part = pull(query_f, query_r, query_gain, dq_all[...])
    grad_ref[:, ROWS : 2 * ROWS], key_part = pull(key_f, key_r, key_gain, dk_acc[...])
    grad_ref[:, 2 * ROWS : 3 * ROWS] = dv_acc[...].astype(BF).reshape(GROUPS, ROWS, HEAD)
    gains = jnp.concatenate([query_part, key_part], axis=0)
    if earlier_ref is None:
        gain_out_ref[...] = gains
    else:
        tail = pair_rows(gains + earlier_ref[...])
        for group in range(GROUPS):
            gain_out_ref[group] = tail


def attend(head, fields, d_out, gains, earlier=None):
    extra = () if earlier is None else (earlier,)
    gain_shape = jax.ShapeDtypeStruct((2, HEAD), F32)
    if extra:
        gain_shape = jax.ShapeDtypeStruct((GROUPS, 16, HEAD), BF)
    return pl.pallas_call(
        lambda *refs: attend_kernel(head, *refs),
        out_shape=(
            jax.ShapeDtypeStruct((SEQ, HEAD), BF),
            jax.ShapeDtypeStruct((GROUPS, 3 * ROWS, HEAD), BF),
            gain_shape,
        ),
        in_specs=[whole()] * (3 + len(extra)),
        out_specs=(whole(),) * 3,
        scratch_shapes=[pltpu.VMEM((SEQ, HEAD), F32)] * 3,
        compiler_params=pltpu.CompilerParams(vmem_limit_bytes=40 << 20),
    )(fields, d_out, gains, *extra)


def weigh_kernel(order_ref, *refs):
    blocks, head_refs = refs[:8], refs[8:10]
    out_ref, rows, sems, terms = refs[-4:]
    gather_blocks(order_ref, blocks, rows, sems)
    here = order_ref[8]
    out_t = jnp.concatenate([ref[...].T for ref in head_refs], axis=0)
    for j in range(PARTS):
        term = jnp.dot(out_t, rows[j].reshape(SEQ, 256), preferred_element_type=F32)
        for head in range(2):
            terms[head, j * 256 : (j + 1) * 256] = (
                term[head * HEAD : (head + 1) * HEAD].T.astype(BF)
            )
    for head in range(2):
        for i in range(4):
            for j in range(8):
                at = (j * 4 + i) * BLOCK
                out_ref[i ^ here, j, head * BLOCK : (head + 1) * BLOCK] = terms[
                    head, at : at + BLOCK
                ]


def pair_rows(rows):
    high = rows.astype(BF)
    low = (rows - high.astype(F32)).astype(BF)
    return jnp.concatenate([high, low, jnp.zeros((12, rows.shape[1]), BF)], axis=0)


def weigh(order, blocks, outs):
    return pl.pallas_call(
        weigh_kernel,
        out_shape=jax.ShapeDtypeStruct((4, 8, 2 * BLOCK + 16, HEAD), BF),
        in_specs=[pl.BlockSpec(memory_space=pltpu.SMEM)] + [anywhere()] * 8 + [whole()] * 2,
        out_specs=whole(),
        scratch_shapes=block_scratch() + [pltpu.VMEM((2, PARTS * 256, HEAD), BF)],
        compiler_params=pltpu.CompilerParams(vmem_limit_bytes=40 << 20),
    )(order, *blocks, *outs)


def tail_kernel(terms_ref, tails_ref, out_ref, tail, sem):
    total = sum(tails_ref[group].astype(F32) for group in range(GROUPS))
    rows = pair_rows(total[0:2] + total[2:4])
    for i in range(4):
        for j in range(8):
            tail[i, j] = rows
    copy = pltpu.make_async_copy(tail, out_ref.at[:, :, 2 * BLOCK : 2 * BLOCK + 16], sem)
    copy.start()
    copy.wait()


def add_tail(terms, tails):
    return pl.pallas_call(
        tail_kernel,
        out_shape=jax.ShapeDtypeStruct(terms.shape, terms.dtype),
        in_specs=[anywhere(), whole()],
        out_specs=anywhere(),
        scratch_shapes=[pltpu.VMEM((4, 8, 16, HEAD), BF), pltpu.SemaphoreType.DMA],
        input_output_aliases={0: 0},
    )(terms, tails)


def first_sum_kernel(*refs):
    terms, out_ref = refs[:4], refs[4]
    at = 2 * BLOCK
    for j in range(8):
        total = sum(ref[j].astype(F32) for ref in terms)
        out_ref[j, 0:at] = total[0:at].astype(BF)
        out_ref[j, at : at + 16] = pair_rows(total[at : at + 2] + total[at + 2 : at + 4])


def first_sum(terms):
    return pl.pallas_call(
        first_sum_kernel,
        out_shape=jax.ShapeDtypeStruct((8, 2 * BLOCK + 16, HEAD), BF),
        in_specs=[whole()] * 4,
        out_specs=whole(),
    )(*terms)


def second_sum_kernel(zhi_ref, in_ref, straight_ref, across_ref):
    total = sum(in_ref[j].astype(F32) for j in range(8))
    half = BLOCK // 2
    at = 2 * BLOCK
    gain = total[at : at + 2] + total[at + 2 : at + 4]
    row = jnp.concatenate([gain[0:1], gain[1:2]], axis=1)
    low_here = zhi_ref[0] == 0
    for ref in (straight_ref, across_ref):
        ref[half : half + 8] = jnp.broadcast_to(row, (8, 2 * HEAD))
    for head in range(2):
        lanes = slice(head * HEAD, (head + 1) * HEAD)
        low = total[head * BLOCK : head * BLOCK + half]
        high = total[head * BLOCK + half : (head + 1) * BLOCK]
        straight_ref[0:half, lanes] = jnp.where(low_here, low, high)
        across_ref[0:half, lanes] = jnp.where(low_here, high, low)


def second_sum(zhi, field):
    shape = jax.ShapeDtypeStruct((BLOCK // 2 + 8, 2 * HEAD), F32)
    return pl.pallas_call(
        second_sum_kernel,
        out_shape=(shape, shape),
        in_specs=[pl.BlockSpec(memory_space=pltpu.SMEM), whole()],
        out_specs=(whole(), whole()),
    )(zhi, field)


def spread(columns):
    x = lax.axis_index("x")
    columns = lax.all_to_all(
        jnp.broadcast_to(columns[None], (8,) + columns.shape), "zlo", 0, 0
    )
    for at, bit in ((1, 2), (2, 1)):
        other = moved(columns, x_step(bit))
        columns = jnp.where(
            (x & bit) == 0,
            jnp.stack([columns, other], axis=at),
            jnp.stack([other, columns], axis=at),
        )
    return columns


def local(query_in, key_in, value_in, velocity_grad, velocity_gap, query_gain, key_gain, out_proj):
    core, zhi, y = lax.axis_index("core"), lax.axis_index("zhi"), lax.axis_index("y")
    first, second = prepare(query_in[0], key_in[0], value_in[0])
    own = out_proj.T
    formed = form(
        jnp.stack([core]).astype(jnp.int32),
        velocity_grad[0],
        velocity_gap[0],
        own,
        after(moved(own, core_swap), first, second),
    )

    formed = moved(formed, clip_swap)
    d_velocity = formed[: PARTS * ROWS].reshape(PARTS, ROWS, 256)
    first = moved(after(first, formed), clip_swap)
    blocks = [d_velocity] + [moved(d_velocity, y_step(step)) for step in (1, 3, 2)]
    weight = spread(formed[PARTS * ROWS :]).reshape(-1, 2 * HEAD)
    blocks = blocks + [moved(block, core_swap) for block in blocks]
    from_y = [y, (y + 3) % 4, (y + 1) % 4, (y + 2) % 4]
    order = [core * 4 + at for at in from_y] + [(1 - core) * 4 + at for at in from_y]
    order = jnp.stack(order + [lax.axis_index("x")]).astype(jnp.int32)
    gains = jnp.stack([query_gain, key_gain])
    second = moved(after(second, first), clip_swap)

    first_in = lax.all_to_all(first, ("core", "y"), 0, 0)
    d_out = project(order, blocks, after(weight, first_in))
    first_out, first_grad, first_gain = attend(0, first_in, d_out, gains)
    first_back = lax.all_to_all(first_grad, ("core", "y"), 0, 0)
    second_in = lax.all_to_all(after(second, first_back), ("core", "y"), 0, 0)
    first_back = moved(first_back, clip_swap)
    second_out, second_grad, tails = attend(1, second_in, d_out, gains, first_gain)
    tails = lax.all_to_all(tails, ("core", "y"), 0, 0)
    terms = add_tail(weigh(order, blocks, (first_out, second_out)), tails)
    second_grad = after(second_grad, first_back, terms)
    second_back = lax.all_to_all(second_grad, ("core", "y"), 0, 0)
    second_back = moved(second_back, clip_swap)
    terms = first_sum([terms[0]] + [moved(terms[i], x_step(i)) for i in (1, 2, 3)])
    terms = lax.all_to_all(after(terms, second_back), "zlo", 0, 0)
    straight, across = second_sum(jnp.stack([zhi]).astype(jnp.int32), terms)
    total = moved(straight, clip_swap) + moved(across, clip_cross)
    grad_out_proj = total[: BLOCK // 2].T
    gain_grads = total[BLOCK // 2].reshape(2, HEAD)

    grad_query, grad_key, grad_value = finish(first_back, second_back)
    return (grad_query[None], grad_key[None], grad_value[None], gain_grads, grad_out_proj)


def solution(mesh):
    fine = Mesh(mesh.devices.reshape(SIZES), AXES)
    blk, uly = ("zlo", "x", "core"), ("zhi", "y")
    rows = P(blk, uly, None)
    return jax.shard_map(
        local,
        mesh=fine,
        in_specs=(rows, rows, rows, rows, rows, P(), P(), P(uly, blk)),
        out_specs=(rows, rows, rows, P(), P(uly, blk)),
        check_vma=False,
    )
```

```python
import itertools
import math

import jax
import jax.numpy as jnp
import numpy as np
from jax import lax
from jax.experimental import pallas as pl
from jax.experimental.pallas import tpu as pltpu
from jax.sharding import Mesh, PartitionSpec as P

kl_weight = 0.5
norm_eps = 1e-06

AXES = ("zlo", "x", "core", "zhi", "y")
SIZES = (8, 4, 2, 2, 4)
PLACES = list(itertools.product(*map(range, SIZES)))
BF = jnp.bfloat16
F32 = jnp.float32
HEAD = 128
ROWS = 128
GROUPS = 8
SEQ = GROUPS * ROWS
TILE = 256
BLOCK = 96
PARTS = 12


def moved(field, where):
    number = lambda place: int(np.ravel_multi_index(place, SIZES))
    pairs = [(number(place), number(where(*place))) for place in PLACES]
    return lax.ppermute(field, AXES, pairs)


def moved_where(field, where, chosen):
    number = lambda place: int(np.ravel_multi_index(place, SIZES))
    pairs = [(number(place), number(where(*place))) for place in PLACES if chosen(*place)]
    return lax.ppermute(field, AXES, pairs)


def clip_swap(l, x, c, h, y):
    return (l, x, h, c, y)


def z_swap(l, x, c, h, y):
    return (l, x, c, 1 - h, y)


def core_swap(l, x, c, h, y):
    return (l, x, 1 - c, h, y)


def y_step(step):
    return lambda l, x, c, h, y: (l, x, c, h, (y + step) % 4)


def x_step(step):
    return lambda l, x, c, h, y: (l, x ^ step, c, h, y)


def z_pair(step):
    return lambda l, x, c, h, y: (l ^ step, x, c, h, y)


def whole():
    return pl.BlockSpec(memory_space=pltpu.VMEM)


def anywhere():
    return pl.BlockSpec(memory_space=pl.ANY)


def after(field, *earlier):
    return pl.pallas_call(
        lambda *refs: None,
        out_shape=jax.ShapeDtypeStruct(field.shape, field.dtype),
        in_specs=[anywhere()] * (1 + len(earlier)),
        out_specs=anywhere(),
        input_output_aliases={0: 0},
    )(field, *earlier)


def prepare_kernel(query_ref, key_ref, value_ref, first_ref, second_ref):
    for part, ref in enumerate((query_ref, key_ref, value_ref)):
        for group in range(GROUPS):
            at = group * 2 * HEAD
            first_ref[group, part] = ref[:, at : at + HEAD]
            second_ref[group, part] = ref[:, at + HEAD : at + 2 * HEAD]


def prepare(query, key, value):
    shape = jax.ShapeDtypeStruct((GROUPS, 3, ROWS, HEAD), BF)
    return pl.pallas_call(
        prepare_kernel,
        out_shape=(shape, shape),
        in_specs=[whole()] * 3,
        out_specs=(whole(), whole()),
    )(query, key, value)


def finish_kernel(first_ref, second_ref, query_ref, key_ref, value_ref):
    for part, ref in enumerate((query_ref, key_ref, value_ref)):
        rows = slice(part * ROWS, (part + 1) * ROWS)
        for group in range(GROUPS):
            at = group * 2 * HEAD
            ref[:, at : at + HEAD] = first_ref[group, rows]
            ref[:, at + HEAD : at + 2 * HEAD] = second_ref[group, rows]


def finish(first, second):
    shape = jax.ShapeDtypeStruct((ROWS, GROUPS * 2 * HEAD), BF)
    return pl.pallas_call(
        finish_kernel,
        out_shape=(shape,) * 3,
        in_specs=[whole()] * 2,
        out_specs=(whole(),) * 3,
    )(first, second)


def form_kernel(core_ref, grad_ref, gap_ref, own_ref, other_ref, out_ref):
    for j in range(PARTS):
        at = slice(j * 256, (j + 1) * 256)
        out_ref[j * ROWS : (j + 1) * ROWS] = (
            grad_ref[:, at].astype(F32) + kl_weight * gap_ref[:, at].astype(F32)
        ).astype(BF)
    half = BLOCK // 2
    core = core_ref[0]
    own_at = pl.multiple_of(PARTS * ROWS + core * half, 16)
    other_at = pl.multiple_of(PARTS * ROWS + (1 - core) * half, 16)
    out_ref[pl.ds(own_at, half)] = own_ref[...]
    out_ref[pl.ds(other_at, half)] = other_ref[...]


def form(core, grad, gap, own, other):
    return pl.pallas_call(
        form_kernel,
        out_shape=jax.ShapeDtypeStruct((PARTS * ROWS + BLOCK, 256), BF),
        in_specs=[pl.BlockSpec(memory_space=pltpu.SMEM)] + [whole()] * 4,
        out_specs=whole(),
    )(core, grad, gap, own, other)


def gather_blocks(order_ref, blocks, rows, sems):
    copies = [
        pltpu.make_async_copy(blocks[i], rows.at[:, order_ref[i]], sems.at[i]) for i in range(8)
    ]
    for copy in copies:
        copy.start()
    for copy in copies:
        copy.wait()


def block_scratch():
    return [pltpu.VMEM((PARTS, GROUPS, ROWS, 256), BF), pltpu.SemaphoreType.DMA((8,))]


def project_kernel(order_ref, *refs):
    blocks, weight_ref, out_ref, rows, sems = refs[:8], refs[8], refs[9], refs[10], refs[11]
    gather_blocks(order_ref, blocks, rows, sems)
    for pair in range(4):
        total = None
        for j in range(PARTS):
            part = jnp.dot(
                rows[j, 2 * pair : 2 * pair + 2].reshape(2 * ROWS, 256),
                weight_ref[j * 256 : (j + 1) * 256],
                preferred_element_type=F32,
            )
            total = part if total is None else total + part
        out = total.astype(BF)
        at = pair * 2 * ROWS
        for head in range(2):
            out_ref[head, at : at + 2 * ROWS] = out[:, head * HEAD : (head + 1) * HEAD]


def project(order, blocks, weight):
    return pl.pallas_call(
        project_kernel,
        out_shape=jax.ShapeDtypeStruct((2, SEQ, HEAD), BF),
        in_specs=[pl.BlockSpec(memory_space=pltpu.SMEM)] + [anywhere()] * 8 + [whole()],
        out_specs=whole(),
        scratch_shapes=block_scratch(),
        compiler_params=pltpu.CompilerParams(vmem_limit_bytes=40 << 20),
    )(order, *blocks, weight)


def attend_kernel(head, *refs):
    in_ref, d_out_ref, gain_ref = refs[:3]
    earlier_ref = refs[3] if len(refs) == 10 else None
    out_ref, grad_ref, gain_out_ref, dk_acc, dv_acc, dq_all = refs[-6:]
    scale = 1.0 / math.sqrt(HEAD)
    query_f = in_ref[:, 0].reshape(SEQ, HEAD).astype(F32)
    key_f = in_ref[:, 1].reshape(SEQ, HEAD).astype(F32)
    value = in_ref[:, 2].reshape(SEQ, HEAD)
    query_gain = gain_ref[0:1]
    key_gain = gain_ref[1:2]
    query_r = lax.rsqrt(jnp.mean(query_f * query_f, axis=-1, keepdims=True) + norm_eps)
    key_r = lax.rsqrt(jnp.mean(key_f * key_f, axis=-1, keepdims=True) + norm_eps)
    query_n = (query_f * query_r * query_gain).astype(BF)
    key_n = (key_f * key_r * key_gain).astype(BF)
    key_t = key_n.T
    value_t = value.T
    for tile in range(SEQ // TILE):
        at = tile * TILE
        query_tile = query_n[at : at + TILE]
        d_out = d_out_ref[head, at : at + TILE]
        d_out_t = d_out.T
        scores = jnp.dot(key_n, query_tile.T, preferred_element_type=F32) * scale
        top = jnp.max(scores, axis=0, keepdims=True)
        terms = jnp.exp(scores - top)
        weights = terms * (1.0 / jnp.sum(terms, axis=0, keepdims=True))
        weights_b = weights.astype(BF)
        out_t = jnp.dot(value_t, weights_b, preferred_element_type=F32).astype(BF)
        delta = jnp.sum(d_out_t.astype(F32) * out_t.astype(F32), axis=0, keepdims=True)
        d_weights = jnp.dot(value, d_out_t, preferred_element_type=F32)
        d_scores = (weights * (d_weights - delta)).astype(BF)
        d_query_t = jnp.dot(key_t, d_scores, preferred_element_type=F32)
        d_key = jnp.dot(d_scores, query_tile, preferred_element_type=F32)
        d_value = jnp.dot(weights_b, d_out, preferred_element_type=F32)
        out_ref[at : at + TILE] = out_t.T
        dq_all[at : at + TILE] = d_query_t.T
        if tile == 0:
            dk_acc[...] = d_key
            dv_acc[...] = d_value
        else:
            dk_acc[...] += d_key
            dv_acc[...] += d_value

    def pull(field, r, gain, cotangent):
        cotangent = cotangent * scale
        scaled = field * r
        gained = cotangent * gain
        inner = jnp.mean(gained * scaled, axis=-1, keepdims=True)
        grad = (r * (gained - scaled * inner)).astype(BF)
        return grad.reshape(GROUPS, ROWS, HEAD), jnp.sum(cotangent * scaled, axis=0, keepdims=True)

    grad_ref[:, 0:ROWS], query_part = pull(query_f, query_r, query_gain, dq_all[...])
    grad_ref[:, ROWS : 2 * ROWS], key_part = pull(key_f, key_r, key_gain, dk_acc[...])
    grad_ref[:, 2 * ROWS : 3 * ROWS] = dv_acc[...].astype(BF).reshape(GROUPS, ROWS, HEAD)
    gains = jnp.concatenate([query_part, key_part], axis=0)
    if earlier_ref is None:
        gain_out_ref[...] = gains
    else:
        tail = pair_rows(gains + earlier_ref[...])
        for group in range(GROUPS):
            gain_out_ref[group] = tail


def attend(head, fields, d_out, gains, earlier=None):
    extra = () if earlier is None else (earlier,)
    gain_shape = jax.ShapeDtypeStruct((2, HEAD), F32)
    if extra:
        gain_shape = jax.ShapeDtypeStruct((GROUPS, 16, HEAD), BF)
    return pl.pallas_call(
        lambda *refs: attend_kernel(head, *refs),
        out_shape=(
            jax.ShapeDtypeStruct((SEQ, HEAD), BF),
            jax.ShapeDtypeStruct((GROUPS, 3 * ROWS, HEAD), BF),
            gain_shape,
        ),
        in_specs=[whole()] * (3 + len(extra)),
        out_specs=(whole(),) * 3,
        scratch_shapes=[pltpu.VMEM((SEQ, HEAD), F32)] * 3,
        compiler_params=pltpu.CompilerParams(vmem_limit_bytes=40 << 20),
    )(fields, d_out, gains, *extra)


def weigh_kernel(order_ref, *refs):
    blocks, head_refs = refs[:8], refs[8:10]
    out_ref, rows, sems, terms = refs[-4:]
    gather_blocks(order_ref, blocks, rows, sems)
    here = order_ref[8]
    out_t = jnp.concatenate([ref[...].T for ref in head_refs], axis=0)
    for j in range(PARTS):
        term = jnp.dot(out_t, rows[j].reshape(SEQ, 256), preferred_element_type=F32)
        for head in range(2):
            terms[head, j * 256 : (j + 1) * 256] = (
                term[head * HEAD : (head + 1) * HEAD].T.astype(BF)
            )
    for head in range(2):
        for i in range(4):
            for j in range(8):
                at = (j * 4 + i) * BLOCK
                out_ref[i ^ here, j, head * BLOCK : (head + 1) * BLOCK] = terms[
                    head, at : at + BLOCK
                ]


def pair_rows(rows):
    high = rows.astype(BF)
    low = (rows - high.astype(F32)).astype(BF)
    return jnp.concatenate([high, low, jnp.zeros((12, rows.shape[1]), BF)], axis=0)


def weigh(order, blocks, outs):
    return pl.pallas_call(
        weigh_kernel,
        out_shape=jax.ShapeDtypeStruct((4, 8, 2 * BLOCK + 16, HEAD), BF),
        in_specs=[pl.BlockSpec(memory_space=pltpu.SMEM)] + [anywhere()] * 8 + [whole()] * 2,
        out_specs=whole(),
        scratch_shapes=block_scratch() + [pltpu.VMEM((2, PARTS * 256, HEAD), BF)],
        compiler_params=pltpu.CompilerParams(vmem_limit_bytes=40 << 20),
    )(order, *blocks, *outs)


def tail_kernel(terms_ref, tails_ref, out_ref, tail, sem):
    total = sum(tails_ref[group].astype(F32) for group in range(GROUPS))
    rows = pair_rows(total[0:2] + total[2:4])
    for i in range(4):
        for j in range(8):
            tail[i, j] = rows
    copy = pltpu.make_async_copy(tail, out_ref.at[:, :, 2 * BLOCK : 2 * BLOCK + 16], sem)
    copy.start()
    copy.wait()


def add_tail(terms, tails):
    return pl.pallas_call(
        tail_kernel,
        out_shape=jax.ShapeDtypeStruct(terms.shape, terms.dtype),
        in_specs=[anywhere(), whole()],
        out_specs=anywhere(),
        scratch_shapes=[pltpu.VMEM((4, 8, 16, HEAD), BF), pltpu.SemaphoreType.DMA],
        input_output_aliases={0: 0},
    )(terms, tails)


def first_sum_kernel(*refs):
    terms, out_ref = refs[:4], refs[4]
    at = 2 * BLOCK
    for j in range(8):
        total = sum(ref[j].astype(F32) for ref in terms)
        out_ref[j, 0:at] = total[0:at].astype(BF)
        out_ref[j, at : at + 16] = pair_rows(total[at : at + 2] + total[at + 2 : at + 4])


def first_sum(terms):
    return pl.pallas_call(
        first_sum_kernel,
        out_shape=jax.ShapeDtypeStruct((8, 2 * BLOCK + 16, HEAD), BF),
        in_specs=[whole()] * 4,
        out_specs=whole(),
    )(*terms)


def second_sum_kernel(in_ref, out_ref):
    total = sum(in_ref[j].astype(F32) for j in range(8))
    half = BLOCK // 2
    at = 2 * BLOCK
    gain = total[at : at + 2] + total[at + 2 : at + 4]
    row = jnp.concatenate([gain[0:1], gain[1:2]], axis=1)
    for part in range(2):
        for head in range(2):
            rows = head * BLOCK + part * half
            out_ref[part, 0:half, head * HEAD : (head + 1) * HEAD] = total[rows : rows + half]
        out_ref[part, half : half + 8] = jnp.broadcast_to(row, (8, 2 * HEAD))


def second_sum(field):
    return pl.pallas_call(
        second_sum_kernel,
        out_shape=jax.ShapeDtypeStruct((2, BLOCK // 2 + 8, 2 * HEAD), F32),
        in_specs=[whole()],
        out_specs=whole(),
    )(field)


def spread(columns):
    x = lax.axis_index("x")
    columns = lax.all_to_all(
        jnp.broadcast_to(columns[None], (8,) + columns.shape), "zlo", 0, 0
    )
    for at, bit in ((1, 2), (2, 1)):
        other = moved(columns, x_step(bit))
        columns = jnp.where(
            (x & bit) == 0,
            jnp.stack([columns, other], axis=at),
            jnp.stack([other, columns], axis=at),
        )
    return columns


def local(query_in, key_in, value_in, velocity_grad, velocity_gap, query_gain, key_gain, out_proj):
    core, zhi, y = lax.axis_index("core"), lax.axis_index("zhi"), lax.axis_index("y")
    first_raw, second = prepare(query_in[0], key_in[0], value_in[0])
    own = out_proj.T
    formed = form(
        jnp.stack([core]).astype(jnp.int32),
        velocity_grad[0],
        velocity_gap[0],
        own,
        moved(own, core_swap),
    )

    formed = moved(formed, clip_swap)
    d_velocity = formed[: PARTS * ROWS].reshape(PARTS, ROWS, 256)
    first = moved(after(first_raw, formed), clip_swap)
    blocks = [d_velocity] + [moved(d_velocity, y_step(step)) for step in (1, 3, 2)]
    weight = spread(after(formed[PARTS * ROWS :], first_raw)).reshape(-1, 2 * HEAD)
    blocks = blocks + [moved(block, core_swap) for block in blocks]
    from_y = [y, (y + 3) % 4, (y + 1) % 4, (y + 2) % 4]
    order = [core * 4 + at for at in from_y] + [(1 - core) * 4 + at for at in from_y]
    order = jnp.stack(order + [lax.axis_index("x")]).astype(jnp.int32)
    gains = jnp.stack([query_gain, key_gain])
    second = moved(after(second, first), clip_swap)

    first_in = lax.all_to_all(first, ("core", "y"), 0, 0)
    d_out = project(order, blocks, after(weight, first_in))
    first_out, first_grad, first_gain = attend(0, first_in, d_out, gains)
    first_back = lax.all_to_all(first_grad, ("core", "y"), 0, 0)
    second_in = lax.all_to_all(after(second, first_back), ("core", "y"), 0, 0)
    first_back = moved(first_back, clip_swap)
    second_out, second_grad, tails = attend(1, second_in, d_out, gains, first_gain)
    tails = lax.all_to_all(tails, ("core", "y"), 0, 0)
    terms = add_tail(weigh(order, blocks, (first_out, second_out)), tails)
    terms = after(terms, first_back)
    second_back = lax.all_to_all(second_grad, ("core", "y"), 0, 0)
    second_back = moved(after(second_back, terms), clip_swap)
    terms = first_sum([terms[0]] + [moved(terms[i], x_step(i)) for i in (1, 2, 3)])
    terms = lax.all_to_all(after(terms, second_back), "zlo", 0, 0)
    total = second_sum(terms)
    total = total + moved_where(total, z_swap, lambda l, x, c, h, y: c != h)
    mine = jnp.where(core == 0, total[0], total[1])
    other = moved(jnp.where(core == 0, total[1], total[0]), core_swap)
    total = jnp.where(core == zhi, mine, other)
    grad_out_proj = total[: BLOCK // 2].T
    gain_grads = total[BLOCK // 2].reshape(2, HEAD)

    grad_query, grad_key, grad_value = finish(first_back, second_back)
    return (grad_query[None], grad_key[None], grad_value[None], gain_grads, grad_out_proj)


def solution(mesh):
    fine = Mesh(mesh.devices.reshape(SIZES), AXES)
    blk, uly = ("zlo", "x", "core"), ("zhi", "y")
    rows = P(blk, uly, None)
    return jax.shard_map(
        local,
        mesh=fine,
        in_specs=(rows, rows, rows, rows, rows, P(), P(), P(uly, blk)),
        out_specs=(rows, rows, rows, P(), P(uly, blk)),
        check_vma=False,
    )
```

```python
import itertools
import math

import jax
import jax.numpy as jnp
import numpy as np
from jax import lax
from jax.experimental import pallas as pl
from jax.experimental.pallas import tpu as pltpu
from jax.sharding import Mesh, PartitionSpec as P

kl_weight = 0.5
norm_eps = 1e-06

AXES = ("zlo", "x", "core", "zhi", "y")
SIZES = (8, 4, 2, 2, 4)
PLACES = list(itertools.product(*map(range, SIZES)))
BF = jnp.bfloat16
F32 = jnp.float32
HEAD = 128
ROWS = 128
GROUPS = 8
SEQ = GROUPS * ROWS
TILE = 256
BLOCK = 96
PARTS = 12


def moved(field, where):
    number = lambda place: int(np.ravel_multi_index(place, SIZES))
    pairs = [(number(place), number(where(*place))) for place in PLACES]
    return lax.ppermute(field, AXES, pairs)


def moved_where(field, where, chosen):
    number = lambda place: int(np.ravel_multi_index(place, SIZES))
    pairs = [(number(place), number(where(*place))) for place in PLACES if chosen(*place)]
    return lax.ppermute(field, AXES, pairs)


def clip_swap(l, x, c, h, y):
    return (l, x, h, c, y)


def z_swap(l, x, c, h, y):
    return (l, x, c, 1 - h, y)


def core_swap(l, x, c, h, y):
    return (l, x, 1 - c, h, y)


def y_step(step):
    return lambda l, x, c, h, y: (l, x, c, h, (y + step) % 4)


def x_step(step):
    return lambda l, x, c, h, y: (l, x ^ step, c, h, y)


def z_pair(step):
    return lambda l, x, c, h, y: (l ^ step, x, c, h, y)


def whole():
    return pl.BlockSpec(memory_space=pltpu.VMEM)


def anywhere():
    return pl.BlockSpec(memory_space=pl.ANY)


def after(field, *earlier):
    return pl.pallas_call(
        lambda *refs: None,
        out_shape=jax.ShapeDtypeStruct(field.shape, field.dtype),
        in_specs=[anywhere()] * (1 + len(earlier)),
        out_specs=anywhere(),
        input_output_aliases={0: 0},
    )(field, *earlier)


def prepare_kernel(query_ref, key_ref, value_ref, first_ref, second_ref):
    for part, ref in enumerate((query_ref, key_ref, value_ref)):
        for group in range(GROUPS):
            at = group * 2 * HEAD
            first_ref[group, part] = ref[:, at : at + HEAD]
            second_ref[group, part] = ref[:, at + HEAD : at + 2 * HEAD]


def prepare(query, key, value):
    shape = jax.ShapeDtypeStruct((GROUPS, 3, ROWS, HEAD), BF)
    return pl.pallas_call(
        prepare_kernel,
        out_shape=(shape, shape),
        in_specs=[whole()] * 3,
        out_specs=(whole(), whole()),
    )(query, key, value)


def finish_kernel(first_ref, second_ref, query_ref, key_ref, value_ref):
    for part, ref in enumerate((query_ref, key_ref, value_ref)):
        rows = slice(part * ROWS, (part + 1) * ROWS)
        for group in range(GROUPS):
            at = group * 2 * HEAD
            ref[:, at : at + HEAD] = first_ref[group, rows]
            ref[:, at + HEAD : at + 2 * HEAD] = second_ref[group, rows]


def finish(first, second):
    shape = jax.ShapeDtypeStruct((ROWS, GROUPS * 2 * HEAD), BF)
    return pl.pallas_call(
        finish_kernel,
        out_shape=(shape,) * 3,
        in_specs=[whole()] * 2,
        out_specs=(whole(),) * 3,
    )(first, second)


def form_kernel(grad_ref, gap_ref, out_ref):
    for j in range(PARTS):
        at = slice(j * 256, (j + 1) * 256)
        out_ref[j * ROWS : (j + 1) * ROWS] = (
            grad_ref[:, at].astype(F32) + kl_weight * gap_ref[:, at].astype(F32)
        ).astype(BF)


def append_kernel(core_ref, formed_ref, own_ref, other_ref, out_ref, sems):
    half = BLOCK // 2
    core = core_ref[0]
    own_at = pl.multiple_of(PARTS * ROWS + core * half, 16)
    other_at = pl.multiple_of(PARTS * ROWS + (1 - core) * half, 16)
    own_copy = pltpu.make_async_copy(own_ref, out_ref.at[pl.ds(own_at, half)], sems.at[0])
    other_copy = pltpu.make_async_copy(other_ref, out_ref.at[pl.ds(other_at, half)], sems.at[1])
    own_copy.start()
    other_copy.start()
    own_copy.wait()
    other_copy.wait()


def form(core, grad, gap, own, other):
    shape = jax.ShapeDtypeStruct((PARTS * ROWS + BLOCK, 256), BF)
    formed = pl.pallas_call(
        form_kernel, out_shape=shape, in_specs=[whole()] * 2, out_specs=whole()
    )(grad, gap)
    return pl.pallas_call(
        append_kernel,
        out_shape=shape,
        in_specs=[pl.BlockSpec(memory_space=pltpu.SMEM), anywhere(), whole(), whole()],
        out_specs=anywhere(),
        scratch_shapes=[pltpu.SemaphoreType.DMA((2,))],
        input_output_aliases={1: 0},
    )(core, formed, own, other)


def gather_blocks(order_ref, blocks, rows, sems):
    copies = [
        pltpu.make_async_copy(blocks[i], rows.at[:, order_ref[i]], sems.at[i]) for i in range(8)
    ]
    for copy in copies:
        copy.start()
    for copy in copies:
        copy.wait()


def block_scratch():
    return [pltpu.VMEM((PARTS, GROUPS, ROWS, 256), BF), pltpu.SemaphoreType.DMA((8,))]


def project_kernel(order_ref, *refs):
    blocks, weight_ref, out_ref, rows, sems = refs[:8], refs[8], refs[9], refs[10], refs[11]
    gather_blocks(order_ref, blocks, rows, sems)
    for pair in range(4):
        total = None
        for j in range(PARTS):
            part = jnp.dot(
                rows[j, 2 * pair : 2 * pair + 2].reshape(2 * ROWS, 256),
                weight_ref[j * 256 : (j + 1) * 256],
                preferred_element_type=F32,
            )
            total = part if total is None else total + part
        out = total.astype(BF)
        at = pair * 2 * ROWS
        for head in range(2):
            out_ref[head, at : at + 2 * ROWS] = out[:, head * HEAD : (head + 1) * HEAD]


def project(order, blocks, weight):
    return pl.pallas_call(
        project_kernel,
        out_shape=jax.ShapeDtypeStruct((2, SEQ, HEAD), BF),
        in_specs=[pl.BlockSpec(memory_space=pltpu.SMEM)] + [anywhere()] * 8 + [whole()],
        out_specs=whole(),
        scratch_shapes=block_scratch(),
        compiler_params=pltpu.CompilerParams(vmem_limit_bytes=40 << 20),
    )(order, *blocks, weight)


def attend_kernel(head, *refs):
    in_ref, d_out_ref, gain_ref = refs[:3]
    earlier_ref = refs[3] if len(refs) == 10 else None
    out_ref, grad_ref, gain_out_ref, dk_acc, dv_acc, dq_all = refs[-6:]
    scale = 1.0 / math.sqrt(HEAD)
    query_f = in_ref[:, 0].reshape(SEQ, HEAD).astype(F32)
    key_f = in_ref[:, 1].reshape(SEQ, HEAD).astype(F32)
    value = in_ref[:, 2].reshape(SEQ, HEAD)
    query_gain = gain_ref[0:1]
    key_gain = gain_ref[1:2]
    query_r = lax.rsqrt(jnp.mean(query_f * query_f, axis=-1, keepdims=True) + norm_eps)
    key_r = lax.rsqrt(jnp.mean(key_f * key_f, axis=-1, keepdims=True) + norm_eps)
    query_n = (query_f * query_r * query_gain).astype(BF)
    key_n = (key_f * key_r * key_gain).astype(BF)
    key_t = key_n.T
    value_t = value.T
    for tile in range(SEQ // TILE):
        at = tile * TILE
        query_tile = query_n[at : at + TILE]
        d_out = d_out_ref[head, at : at + TILE]
        d_out_t = d_out.T
        scores = jnp.dot(key_n, query_tile.T, preferred_element_type=F32) * scale
        top = jnp.max(scores, axis=0, keepdims=True)
        terms = jnp.exp(scores - top)
        weights = terms * (1.0 / jnp.sum(terms, axis=0, keepdims=True))
        weights_b = weights.astype(BF)
        out_t = jnp.dot(value_t, weights_b, preferred_element_type=F32).astype(BF)
        delta = jnp.sum(d_out_t.astype(F32) * out_t.astype(F32), axis=0, keepdims=True)
        d_weights = jnp.dot(value, d_out_t, preferred_element_type=F32)
        d_scores = (weights * (d_weights - delta)).astype(BF)
        d_query_t = jnp.dot(key_t, d_scores, preferred_element_type=F32)
        d_key = jnp.dot(d_scores, query_tile, preferred_element_type=F32)
        d_value = jnp.dot(weights_b, d_out, preferred_element_type=F32)
        out_ref[at : at + TILE] = out_t.T
        dq_all[at : at + TILE] = d_query_t.T
        if tile == 0:
            dk_acc[...] = d_key
            dv_acc[...] = d_value
        else:
            dk_acc[...] += d_key
            dv_acc[...] += d_value

    def pull(field, r, gain, cotangent):
        cotangent = cotangent * scale
        scaled = field * r
        gained = cotangent * gain
        inner = jnp.mean(gained * scaled, axis=-1, keepdims=True)
        grad = (r * (gained - scaled * inner)).astype(BF)
        return grad.reshape(GROUPS, ROWS, HEAD), jnp.sum(cotangent * scaled, axis=0, keepdims=True)

    grad_ref[:, 0:ROWS], query_part = pull(query_f, query_r, query_gain, dq_all[...])
    grad_ref[:, ROWS : 2 * ROWS], key_part = pull(key_f, key_r, key_gain, dk_acc[...])
    grad_ref[:, 2 * ROWS : 3 * ROWS] = dv_acc[...].astype(BF).reshape(GROUPS, ROWS, HEAD)
    gains = jnp.concatenate([query_part, key_part], axis=0)
    if earlier_ref is None:
        gain_out_ref[...] = gains
    else:
        tail = pair_rows(gains + earlier_ref[...])
        for group in range(GROUPS):
            gain_out_ref[group] = tail


def attend(head, fields, d_out, gains, earlier=None):
    extra = () if earlier is None else (earlier,)
    gain_shape = jax.ShapeDtypeStruct((2, HEAD), F32)
    if extra:
        gain_shape = jax.ShapeDtypeStruct((GROUPS, 16, HEAD), BF)
    return pl.pallas_call(
        lambda *refs: attend_kernel(head, *refs),
        out_shape=(
            jax.ShapeDtypeStruct((SEQ, HEAD), BF),
            jax.ShapeDtypeStruct((GROUPS, 3 * ROWS, HEAD), BF),
            gain_shape,
        ),
        in_specs=[whole()] * (3 + len(extra)),
        out_specs=(whole(),) * 3,
        scratch_shapes=[pltpu.VMEM((SEQ, HEAD), F32)] * 3,
        compiler_params=pltpu.CompilerParams(vmem_limit_bytes=40 << 20),
    )(fields, d_out, gains, *extra)


def weigh_kernel(order_ref, *refs):
    blocks, head_refs = refs[:8], refs[8:10]
    out_ref, rows, sems, terms = refs[-4:]
    gather_blocks(order_ref, blocks, rows, sems)
    here = order_ref[8]
    out_t = jnp.concatenate([ref[...].T for ref in head_refs], axis=0)
    for j in range(PARTS):
        term = jnp.dot(out_t, rows[j].reshape(SEQ, 256), preferred_element_type=F32)
        for head in range(2):
            terms[head, j * 256 : (j + 1) * 256] = (
                term[head * HEAD : (head + 1) * HEAD].T.astype(BF)
            )
    for head in range(2):
        for i in range(4):
            for j in range(8):
                at = (j * 4 + i) * BLOCK
                out_ref[i ^ here, j, head * BLOCK : (head + 1) * BLOCK] = terms[
                    head, at : at + BLOCK
                ]


def pair_rows(rows):
    high = rows.astype(BF)
    low = (rows - high.astype(F32)).astype(BF)
    return jnp.concatenate([high, low, jnp.zeros((12, rows.shape[1]), BF)], axis=0)


def weigh(order, blocks, outs):
    return pl.pallas_call(
        weigh_kernel,
        out_shape=jax.ShapeDtypeStruct((4, 8, 2 * BLOCK + 16, HEAD), BF),
        in_specs=[pl.BlockSpec(memory_space=pltpu.SMEM)] + [anywhere()] * 8 + [whole()] * 2,
        out_specs=whole(),
        scratch_shapes=block_scratch() + [pltpu.VMEM((2, PARTS * 256, HEAD), BF)],
        compiler_params=pltpu.CompilerParams(vmem_limit_bytes=40 << 20),
    )(order, *blocks, *outs)


def tail_kernel(terms_ref, tails_ref, out_ref, tail, sem):
    total = sum(tails_ref[group].astype(F32) for group in range(GROUPS))
    rows = pair_rows(total[0:2] + total[2:4])
    for i in range(4):
        for j in range(8):
            tail[i, j] = rows
    copy = pltpu.make_async_copy(tail, out_ref.at[:, :, 2 * BLOCK : 2 * BLOCK + 16], sem)
    copy.start()
    copy.wait()


def add_tail(terms, tails):
    return pl.pallas_call(
        tail_kernel,
        out_shape=jax.ShapeDtypeStruct(terms.shape, terms.dtype),
        in_specs=[anywhere(), whole()],
        out_specs=anywhere(),
        scratch_shapes=[pltpu.VMEM((4, 8, 16, HEAD), BF), pltpu.SemaphoreType.DMA],
        input_output_aliases={0: 0},
    )(terms, tails)


def first_sum_kernel(*refs):
    terms, out_ref = refs[:4], refs[4]
    at = 2 * BLOCK
    for j in range(8):
        total = sum(ref[j].astype(F32) for ref in terms)
        out_ref[j, 0:at] = total[0:at].astype(BF)
        out_ref[j, at : at + 16] = pair_rows(total[at : at + 2] + total[at + 2 : at + 4])


def first_sum(terms):
    return pl.pallas_call(
        first_sum_kernel,
        out_shape=jax.ShapeDtypeStruct((8, 2 * BLOCK + 16, HEAD), BF),
        in_specs=[whole()] * 4,
        out_specs=whole(),
    )(*terms)


def second_sum_kernel(in_ref, out_ref):
    total = sum(in_ref[j].astype(F32) for j in range(8))
    half = BLOCK // 2
    at = 2 * BLOCK
    gain = total[at : at + 2] + total[at + 2 : at + 4]
    row = jnp.concatenate([gain[0:1], gain[1:2]], axis=1)
    for part in range(2):
        for head in range(2):
            rows = head * BLOCK + part * half
            out_ref[part, 0:half, head * HEAD : (head + 1) * HEAD] = total[rows : rows + half]
        out_ref[part, half : half + 8] = jnp.broadcast_to(row, (8, 2 * HEAD))


def second_sum(field):
    return pl.pallas_call(
        second_sum_kernel,
        out_shape=jax.ShapeDtypeStruct((2, BLOCK // 2 + 8, 2 * HEAD), F32),
        in_specs=[whole()],
        out_specs=whole(),
    )(field)


def spread(columns):
    x = lax.axis_index("x")
    columns = lax.all_to_all(
        jnp.broadcast_to(columns[None], (8,) + columns.shape), "zlo", 0, 0
    )
    for at, bit in ((1, 2), (2, 1)):
        other = moved(columns, x_step(bit))
        columns = jnp.where(
            (x & bit) == 0,
            jnp.stack([columns, other], axis=at),
            jnp.stack([other, columns], axis=at),
        )
    return columns


def local(query_in, key_in, value_in, velocity_grad, velocity_gap, query_gain, key_gain, out_proj):
    core, zhi, y = lax.axis_index("core"), lax.axis_index("zhi"), lax.axis_index("y")
    first_raw, second = prepare(query_in[0], key_in[0], value_in[0])
    own = out_proj.T
    formed = form(
        jnp.stack([core]).astype(jnp.int32),
        velocity_grad[0],
        velocity_gap[0],
        own,
        moved(own, core_swap),
    )

    formed = moved(formed, clip_swap)
    d_velocity = formed[: PARTS * ROWS].reshape(PARTS, ROWS, 256)
    first = moved(after(first_raw, formed), clip_swap)
    blocks = [d_velocity] + [moved(d_velocity, y_step(step)) for step in (1, 3, 2)]
    weight = spread(after(formed[PARTS * ROWS :], first_raw)).reshape(-1, 2 * HEAD)
    blocks = blocks + [moved(block, core_swap) for block in blocks]
    from_y = [y, (y + 3) % 4, (y + 1) % 4, (y + 2) % 4]
    order = [core * 4 + at for at in from_y] + [(1 - core) * 4 + at for at in from_y]
    order = jnp.stack(order + [lax.axis_index("x")]).astype(jnp.int32)
    gains = jnp.stack([query_gain, key_gain])
    second = moved(after(second, first), clip_swap)

    first_in = lax.all_to_all(first, ("core", "y"), 0, 0)
    d_out = project(order, blocks, after(weight, first_in))
    first_out, first_grad, first_gain = attend(0, first_in, d_out, gains)
    first_back = lax.all_to_all(first_grad, ("core", "y"), 0, 0)
    second_in = lax.all_to_all(after(second, first_back), ("core", "y"), 0, 0)
    first_back = moved(first_back, clip_swap)
    second_out, second_grad, tails = attend(1, second_in, d_out, gains, first_gain)
    tails = lax.all_to_all(tails, ("core", "y"), 0, 0)
    terms = add_tail(weigh(order, blocks, (first_out, second_out)), tails)
    terms = after(terms, first_back)
    second_back = lax.all_to_all(second_grad, ("core", "y"), 0, 0)
    second_back = moved(after(second_back, terms), clip_swap)
    terms = first_sum([terms[0]] + [moved(terms[i], x_step(i)) for i in (1, 2, 3)])
    terms = lax.all_to_all(after(terms, second_back), "zlo", 0, 0)
    total = second_sum(terms)
    total = total + moved_where(total, z_swap, lambda l, x, c, h, y: c != h)
    mine = jnp.where(core == 0, total[0], total[1])
    other = moved(jnp.where(core == 0, total[1], total[0]), core_swap)
    total = jnp.where(core == zhi, mine, other)
    grad_out_proj = total[: BLOCK // 2].T
    gain_grads = total[BLOCK // 2].reshape(2, HEAD)

    grad_query, grad_key, grad_value = finish(first_back, second_back)
    return (grad_query[None], grad_key[None], grad_value[None], gain_grads, grad_out_proj)


def solution(mesh):
    fine = Mesh(mesh.devices.reshape(SIZES), AXES)
    blk, uly = ("zlo", "x", "core"), ("zhi", "y")
    rows = P(blk, uly, None)
    return jax.shard_map(
        local,
        mesh=fine,
        in_specs=(rows, rows, rows, rows, rows, P(), P(), P(uly, blk)),
        out_specs=(rows, rows, rows, P(), P(uly, blk)),
        check_vma=False,
    )
```
